256 devices in a mesh: member: 16 (over y, x), region: 16 (over z, core).
Axes of the slice: x: 4, y: 4, z: 8, core: 2. Of those that a mesh axis runs over, the one named last changes fastest.
Arguments:
- states: float32 [256, 393216], P('member', 'region'), may hold values from -6 to 6
- weights: float32 [256, 393216], P('member', 'region'), may hold values from -6 to 6
- obs_count: int32 [3072], P('region'), may hold values from 0 to 32
- neighbours: int32 [3072, 12], P('region'), may hold values from 0 to 3071, as said below
Outputs:
- increments: float32 [256, 393216], P('member', 'region')
The draws below stay inside these ranges and needn't reach their ends.
Inputs may be any that keep to these rules, and one draw needn't show every extreme that they name: `neighbours`: each row lists 12 distinct tiles, all within 8 tiles of its own tile counting cyclically over the 3072 tiles; the list always holds the tile itself and the tiles exactly 8 before and after it, in a drawn order.
All inputs are finite; a program needn't handle non-finite values.
Results may differ from the reference program's by a relative error of at most 0.0003.
Values sent between devices are 32-bit elements; how exact they have to be, the bound alone decides.
No kernel may reach another device: no remote copies, remote signals or barrier semaphores. Data moves between devices by JAX's collectives and lax.ppermute only.
A program may use at most 128 MiB of HBM per device.

```python
import jax
import jax.numpy as jnp
from jax import lax

M = 256
TILE = 128
NEIGHBOURS = 12
HALO_TILES = 8
TPD = 12
TILES = 3072
ROWS = 393216


def draw_neighbours(key, part):
    spread = jnp.concatenate([jnp.arange(-HALO_TILES + 1, 0, dtype=jnp.int32), jnp.arange(1, HALO_TILES, dtype=jnp.int32)])
    fixed_part = jnp.array([0, -HALO_TILES, HALO_TILES], dtype=jnp.int32)
    picks = NEIGHBOURS - 3
    keys = jax.random.split(jax.random.fold_in(key, 7), TILES)

    def one_tile(tile_key):
        first_key, second_key = jax.random.split(tile_key)
        chosen = spread[jax.random.permutation(first_key, spread.shape[0])[:picks]]
        offsets = jnp.concatenate([fixed_part, chosen])
        return offsets[jax.random.permutation(second_key, NEIGHBOURS)]
    offsets = jax.vmap(one_tile)(keys)
    tiles_here = jnp.arange(TILES, dtype=jnp.int32)[:, None]
    return ((tiles_here + offsets) % TILES).astype(jnp.int32)


def place_ends(values, key, low, high):
    spot = [jax.random.randint(jax.random.fold_in(key, axis), (), 0, length) for axis, length in enumerate(values.shape)]
    longest = values.shape.index(max(values.shape))
    next_to = spot[:longest] + [(spot[longest] + 1) % values.shape[longest]] + spot[longest + 1:]
    return values.at[tuple(spot)].set(low).at[tuple(next_to)].set(high)


def level_of(own_key, dims, shards, low, top_value):
    loudness, own = 1.0, jax.random.fold_in(own_key, 6)
    for dim, shards_of in shards:
        steps = jnp.exp(jax.random.uniform(jax.random.fold_in(own, dim), (shards_of,), jnp.float32, low / len(shards), top_value / len(shards)))
        loudness = loudness * jnp.repeat(steps, dims[dim] // shards_of).reshape([-1 if axis == dim else 1 for axis in range(len(dims))])
    return loudness


def bell_draw(stream_key, extent, deviation, reach, cuts=(), kind=jnp.bfloat16):
    loudness = level_of(stream_key, extent, cuts, -0.22, 0.18) if cuts else 1.0
    drawn = jax.random.normal(stream_key, extent, jnp.float32) * deviation * loudness
    return jnp.minimum(jnp.maximum(drawn, -reach), reach).astype(kind)


def setup_inputs(seed: int = 0) -> dict:
    splits = jax.random.split(jax.random.key(seed), 5)
    states = bell_draw(splits[0], (M, ROWS), 1.0, 6.0, ((0, 16), (1, 16)), jnp.float32)
    weights = bell_draw(splits[1], (M, ROWS), 1.0, 6.0, ((0, 16), (1, 16)), jnp.float32)
    obs_count = place_ends(jax.random.randint(splits[2], (TILES,), 0, 33), jax.random.fold_in(splits[2], 1), 0, 32).astype(jnp.int32)
    neighbours = draw_neighbours(jax.random.fold_in(splits[4], 71), 0)
    return {"states": states, "weights": weights, "obs_count": obs_count, "neighbours": neighbours}


def taper(offset, tile):
    rows = jnp.arange(tile, dtype=jnp.float32)
    spread = tile * offset[:, None, None] + rows[None, None, :] - rows[None, :, None]
    scaled = spread / (2.0 * tile)
    return 1.0 / (1.0 + scaled * scaled)


def reference(states, weights, obs_count, neighbours):
    members = states.shape[0]
    counts = obs_count.astype(jnp.float32)
    factor = counts / (counts + 8.0)
    state_rows = states.T
    weight_rows = weights.T
    anomaly = state_rows - jnp.mean(state_rows, axis=1, keepdims=True)
    scaled = weight_rows.reshape(TILES, TILE, members) * factor[:, None, None]
    blocks = anomaly.reshape(TILES, TILE, members)

    def group(first):
        own = first + jnp.arange(TPD, dtype=jnp.int32)
        mine = lax.dynamic_slice_in_dim(blocks, first, TPD, 0)
        lists = lax.dynamic_slice_in_dim(neighbours, first, TPD, 0)
        total = jnp.zeros((TPD, TILE, members), jnp.float32)
        for slot in range(NEIGHBOURS):
            chosen = lists[:, slot].astype(jnp.int32)
            offset = ((chosen - own + TILES // 2) % TILES - TILES // 2).astype(jnp.float32)
            others = blocks[chosen]
            other_weights = scaled[chosen]
            covar = jnp.einsum("tim,tjm->tij", mine, others, precision=lax.Precision.HIGHEST) / (members - 1.0)
            total = total + jnp.einsum("tij,tjm->tim", taper(offset, TILE) * covar, other_weights, precision=lax.Precision.HIGHEST)
        return total

    starts = jnp.arange(TILES // TPD, dtype=jnp.int32) * TPD
    result = lax.map(group, starts)
    return result.reshape(ROWS, members).T
```

```python
import jax
import jax.numpy as jnp
from jax import lax
from jax.experimental import pallas as pl
from jax.experimental.pallas import tpu as pltpu
from jax.sharding import PartitionSpec as P

TILE = 128
HALO = 8
OWN = 12
CHIP = 2 * OWN
PART = (CHIP + 2 * HALO) // 2
WINDOW = OWN + 2 * HALO
PAIRS = OWN // 2
SPAN = 2 * HALO + 2
BF = jnp.bfloat16
F32 = jnp.float32


def split(x):
    high = x.astype(BF)
    return high, (x - high.astype(F32)).astype(BF)


def dot(a, b):
    return jnp.dot(a, b, preferred_element_type=F32)


def enkf_kernel(core_ref, mask_ref, mine_ref, other_ref, out_ref, ath, atl, ah, al, wh, wl, taper, ch, cl):
    core = core_ref[0]
    members = out_ref.shape[0]

    def place(ref, t, w):
        lanes = pl.ds(pl.multiple_of(t * TILE, TILE), TILE)
        there = pl.ds(pl.multiple_of(w * TILE, TILE), TILE)
        state = ref[:, 0, :, lanes].reshape(members, TILE)
        anomaly = state - jnp.sum(state, axis=0, keepdims=True) * (1.0 / members)
        ah[:, there], al[:, there] = split(anomaly)
        ath[there, :], atl[there, :] = split(anomaly.T)
        wh[:, there], wl[:, there] = split(ref[:, 1, :, lanes].reshape(members, TILE))

    @pl.loop(0, PART)
    def _(t):
        first = t < OWN
        w = jnp.where(core == 0, t, jnp.where(first, t + 16, t - 4))
        place(mine_ref, t, w)

    @pl.loop(0, HALO)
    def _(t):
        place(other_ref, t, t + 20 * (1 - core))

    @pl.loop(0, SPAN)
    def _(k):
        rows = lax.broadcasted_iota(jnp.int32, (TILE, 2 * TILE), 0)
        columns = lax.broadcasted_iota(jnp.int32, (TILE, 2 * TILE), 1)
        scaled = (rows - columns + (k - HALO) * TILE).astype(F32) / (2.0 * TILE)
        taper[pl.ds(pl.multiple_of(k * TILE, TILE), TILE), :] = 1.0 / (1.0 + scaled * scaled)

    @pl.loop(0, PAIRS)
    def _(pair):
        first = pl.multiple_of(pair * 2 * TILE, 2 * TILE)
        band = pl.ds(first, SPAN * TILE)
        own = pl.ds(pl.multiple_of(first + HALO * TILE, 2 * TILE), 2 * TILE)
        own_high, own_low = ah[:, own], al[:, own]
        for k in range(0, SPAN, 2):
            rows = pl.ds(pl.multiple_of(first + k * TILE, 2 * TILE), 2 * TILE)
            high = ath[rows, :]
            covar = dot(high, own_high) + (dot(atl[rows, :], own_high) + dot(high, own_low))
            covar = covar * taper[k * TILE : (k + 2) * TILE, :]
            for half in range(2):
                keep = mask_ref[pl.ds(pair * SPAN + k + half, 1), :]
                coefficient = covar[half * TILE : (half + 1) * TILE] * keep
                spot = slice((k + half) * TILE, (k + half + 1) * TILE)
                ch[spot, :], cl[spot, :] = split(coefficient)
        out_ref[:, pl.ds(first, 2 * TILE)] = dot(wh[:, band], ch[...]) + (
            dot(wl[:, band], ch[...]) + dot(wh[:, band], cl[...])
        )


def increments_of(core, mask, mine, other):
    members = mine.shape[0] * mine.shape[2]
    vmem = pl.BlockSpec(memory_space=pltpu.VMEM)
    return pl.pallas_call(
        enkf_kernel,
        out_shape=jax.ShapeDtypeStruct((members, OWN * TILE), F32),
        in_specs=[pl.BlockSpec(memory_space=pltpu.SMEM), vmem, vmem, vmem],
        out_specs=vmem,
        scratch_shapes=[
            pltpu.VMEM((WINDOW * TILE, members), BF),
            pltpu.VMEM((WINDOW * TILE, members), BF),
            pltpu.VMEM((members, WINDOW * TILE), BF),
            pltpu.VMEM((members, WINDOW * TILE), BF),
            pltpu.VMEM((members, WINDOW * TILE), BF),
            pltpu.VMEM((members, WINDOW * TILE), BF),
            pltpu.VMEM((SPAN * TILE, 2 * TILE), F32),
            pltpu.VMEM((SPAN * TILE, 2 * TILE), BF),
            pltpu.VMEM((SPAN * TILE, 2 * TILE), BF),
        ],
        compiler_params=pltpu.CompilerParams(vmem_limit_bytes=48 * 1024 * 1024),
        cost_estimate=pl.CostEstimate(flops=11_000_000_000, bytes_accessed=9_000_000, transcendentals=0),
    )(core, mask, mine, other)


def keep_mask(neighbours, core, chip, half, regions, rest):
    swap = [(r, r ^ 1) for r in range(regions)]
    theirs = lax.ppermute(neighbours, "region", swap)
    table = jnp.where((chip >= half) == (core == 1), neighbours, theirs)
    start = (chip % half) * CHIP + core * OWN
    lists = lax.dynamic_slice_in_dim(table, start, OWN, 0)
    tiles = neighbours.shape[0] * regions
    region = lax.axis_index("region")
    first = ((region // 2) * 2 + chip // half) * neighbours.shape[0] + start
    spot = (lists - first + HALO) % tiles
    own = jnp.arange(OWN, dtype=jnp.int32).reshape(PAIRS, 1, 2)
    window = own[:, :1, :1] + jnp.arange(SPAN, dtype=jnp.int32).reshape(1, SPAN, 1)
    listed = spot.reshape(PAIRS, 1, 2, -1) == window[..., None]
    keep = jnp.any(listed, axis=-1)
    keep = jnp.where(keep, rest, 0.0).astype(F32)
    return jnp.repeat(keep, TILE, axis=2).reshape(PAIRS * SPAN, 2 * TILE)


def shards(states, weights, obs_count, neighbours):
    chips = lax.axis_size("member")
    regions = lax.axis_size("region")
    rows, local = states.shape
    tiles = local // TILE
    half = chips // 2
    core = lax.axis_index("region") % 2
    chip = lax.axis_index("member")
    up = [(r, (r + 1) % regions) for r in range(regions)]
    down = [(t, s) for s, t in up]
    swap = [(r, r ^ 1) for r in range(regions)]
    rim = HALO * TILE
    counts = obs_count.astype(F32)
    factor = counts / (counts + 8.0)
    scaled = (weights.reshape(rows, tiles, TILE) * factor[None, :, None]).reshape(rows, local)
    stacked = jnp.stack([states, scaled])
    low = lax.ppermute(stacked[:, :, local - rim :], "region", up)
    high = lax.ppermute(stacked[:, :, :rim], "region", down)
    padded = jnp.concatenate([low, stacked, high], axis=2)

    def windows(side):
        if side == 0:
            spans = [(0, PART)]
        else:
            spans = [(PART + HALO, 2 * PART), (PART, PART + HALO)]
        parts = []
        for q in range(half):
            pieces = [padded[:, :, (q * CHIP + a) * TILE : (q * CHIP + b) * TILE] for a, b in spans]
            parts.append(jnp.concatenate(pieces, axis=2) if len(pieces) > 1 else pieces[0])
        return jnp.stack(parts)

    left, right = windows(0), windows(1)
    is_left = core == 0
    keep_here = jnp.where(is_left, left, right)
    send = jnp.where(is_left, right, left)
    got = lax.ppermute(send, "region", swap)
    lower = jnp.where(is_left, keep_here, got)
    upper = jnp.where(is_left, got, keep_here)
    operand = jnp.concatenate([lower, upper], axis=0)
    mine = lax.all_to_all(operand, "member", split_axis=0, concat_axis=0, tiled=True)
    other = lax.ppermute(mine[:, :, :, OWN * TILE :], "region", swap)
    members = chips * rows
    mask = keep_mask(neighbours, core, chip, half, regions, 1.0 / (members - 1.0))
    total = increments_of(core.reshape(1), mask, mine, other)
    back = lax.all_to_all(
        total.reshape(chips, rows, OWN * TILE), "member", split_axis=0, concat_axis=0, tiled=True
    )
    keep_back = jnp.where(is_left, back[:half], back[half:])
    send_back = jnp.where(is_left, back[half:], back[:half])
    got_back = lax.ppermute(send_back, "region", swap)
    first = jnp.where(is_left, keep_back, got_back)
    second = jnp.where(is_left, got_back, keep_back)
    result = jnp.stack([first, second], axis=1)
    return result.transpose(2, 0, 1, 3).reshape(rows, local)


def solution(mesh):
    placed = (P("member", "region"), P("member", "region"), P("region"), P("region", None))
    return jax.shard_map(
        shards, mesh=mesh, in_specs=placed, out_specs=P("member", "region"), check_vma=False
    )
```

```python
import jax
import jax.numpy as jnp
from jax import lax
from jax.experimental import pallas as pl
from jax.experimental.pallas import tpu as pltpu
from jax.sharding import PartitionSpec as P

TILE = 128
HALO = 8
OWN = 12
CHIP = 2 * OWN
WINDOW = OWN + 2 * HALO
PAIRS = OWN // 2
SPAN = 2 * HALO + 2
BF = jnp.bfloat16
F32 = jnp.float32
MIB = 1024 * 1024
VMEM = pl.BlockSpec(memory_space=pltpu.VMEM)
SMEM = pl.BlockSpec(memory_space=pltpu.SMEM)


def split(x):
    high = x.astype(BF)
    return high, (x - high.astype(F32)).astype(BF)


def dot(a, b):
    return jnp.dot(a, b, preferred_element_type=F32)


def cols(start, count=1):
    return slice(start * TILE, (start + count) * TILE)


def lanes(t, count=1):
    return pl.ds(pl.multiple_of(t * TILE, TILE), count * TILE)


def send_kernel(core_ref, counts_ref, states_ref, weights_ref, scaled_ref, out_ref):
    half = out_ref.shape[0]

    @pl.loop(0, half * CHIP // 8)
    def _(group):
        for lane in range(8):
            t = group * 8 + lane
            count = jnp.full((1, TILE), counts_ref[t], jnp.int32).astype(F32)
            scaled_ref[:, lanes(t)] = weights_ref[:, lanes(t)] * (count / (count + 8.0))

    rows = states_ref.shape[0]
    for ref, there in ((states_ref, slice(0, rows)), (scaled_ref, slice(rows, None))):

        @pl.when(core_ref[0] == 0)
        def _(ref=ref, there=there):
            for q in range(half):
                for t in range(OWN):
                    out_ref[q, there, cols(t)] = ref[:, cols((q + 1) * CHIP - 1 - t)]

        @pl.when(core_ref[0] != 0)
        def _(ref=ref, there=there):
            for q in range(half):
                out_ref[q, there, cols(0, OWN)] = ref[:, cols(q * CHIP, OWN)]


def merge_kernel(core_ref, states_ref, scaled_ref, got_ref, out_ref):
    half = got_ref.shape[0]
    rows = states_ref.shape[0]

    @pl.when(core_ref[0] == 0)
    def _():
        for q in range(half):
            out_ref[q, :rows, :] = states_ref[:, cols(q * CHIP, OWN)]
            out_ref[q, rows:, :] = scaled_ref[:, cols(q * CHIP, OWN)]
            out_ref[half + q] = got_ref[q]

    @pl.when(core_ref[0] != 0)
    def _():
        for q in range(half):
            for t in range(OWN):
                out_ref[half + q, :rows, cols(t)] = states_ref[:, cols((q + 1) * CHIP - 1 - t)]
                out_ref[half + q, rows:, cols(t)] = scaled_ref[:, cols((q + 1) * CHIP - 1 - t)]
            out_ref[q] = got_ref[q]


def place_kernel(core_ref, back_ref, got_ref, out_ref):
    half = got_ref.shape[0]

    @pl.when(core_ref[0] == 0)
    def _():
        for q in range(half):
            out_ref[:, cols(q * CHIP, OWN)] = back_ref[q]
            for t in range(OWN):
                out_ref[:, cols((q + 1) * CHIP - 1 - t)] = got_ref[q, :, cols(t)]

    @pl.when(core_ref[0] != 0)
    def _():
        for q in range(half):
            out_ref[:, cols(q * CHIP, OWN)] = got_ref[q]
            for t in range(OWN):
                out_ref[:, cols((q + 1) * CHIP - 1 - t)] = back_ref[half + q, :, cols(t)]


def anomaly_of(ref, t, members):
    rows = members // ref.shape[0]
    state = ref[:, :rows, lanes(t)].reshape(members, TILE)
    return state - jnp.sum(state, axis=0, keepdims=True) * (1.0 / members)


def place_window(ref, t, w, members, ath, atl, both):
    ath[lanes(w), :], atl[lanes(w), :] = split(anomaly_of(ref, t, members).T)
    weights = ref[:, members // ref.shape[0] :, lanes(t)].reshape(members, TILE)
    both[:members, lanes(w)], both[members:, lanes(w)] = split(weights)


def place_own(ref, t, members, ah, al):
    ah[:, lanes(t)], al[:, lanes(t)] = split(anomaly_of(ref, t, members))


def place_taper(core, count, taper):
    sign = jnp.where(core == 0, TILE, -TILE)

    @pl.loop(0, count)
    def _(k):
        down = lax.broadcasted_iota(jnp.int32, (TILE, 2 * TILE), 0)
        across = lax.broadcasted_iota(jnp.int32, (TILE, 2 * TILE), 1)
        second = (across >= TILE).astype(jnp.int32)
        spread = sign * (k - HALO - second) + down - (across - TILE * second)
        scaled = spread.astype(F32) / (2.0 * TILE)
        taper[lanes(k), :] = 1.0 / (1.0 + scaled * scaled)


def products(pair, first, last, skip, mask_ref, ah, al, ath, atl, both, taper, ch, cl):
    members = ah.shape[0]
    own_high, own_low = ah[:, cols(2 * pair, 2)], al[:, cols(2 * pair, 2)]
    slot = pair % 2
    for k in range(first, last, 2):
        there = cols(2 * pair + k - skip, 2)
        high = ath[there, :]
        covar = dot(high, own_high) + (dot(atl[there, :], own_high) + dot(high, own_low))
        covar = covar * taper[cols(k, 2), :]
        for half in range(2):
            keep = mask_ref[pair * SPAN + k + half : pair * SPAN + k + half + 1, :]
            coefficient = covar[half * TILE : (half + 1) * TILE] * keep
            ch[slot, cols(k + half), :], cl[slot, cols(k + half), :] = split(coefficient)
    band = cols(2 * pair + first - skip, last - first)
    high, low = ch[slot, cols(first, last - first), :], cl[slot, cols(first, last - first), :]
    total = dot(both[:, band], high)
    return total[:members] + (total[members:] + dot(both[:members, band], low))


def near_kernel(core_ref, mask_ref, mine_ref, other_ref, out_ref, ah, al, ath, atl, both, taper, ch, cl):
    members = ah.shape[0]

    @pl.loop(0, OWN)
    def _(t):
        place_window(mine_ref, t, t, members, ath, atl, both)
        place_own(mine_ref, t, members, ah, al)

    @pl.loop(0, HALO)
    def _(t):
        place_window(other_ref, t, OWN + HALO - 1 - t, members, ath, atl, both)

    place_taper(core_ref[0], SPAN, taper)
    for pair in range(PAIRS):
        first = max(0, HALO - 2 * pair)
        out_ref[:, cols(2 * pair, 2)] = products(
            pair, first, SPAN, HALO, mask_ref, ah, al, ath, atl, both, taper, ch, cl
        )


def far_kernel(core_ref, mask_ref, mine_ref, halo_ref, near_ref, out_ref, ah, al, ath, atl, both, taper, ch, cl):
    members = ah.shape[0]

    @pl.loop(0, HALO)
    def _(t):
        place_window(halo_ref, t, HALO - 1 - t, members, ath, atl, both)
        place_own(mine_ref, t, members, ah, al)

    place_taper(core_ref[0], HALO, taper)
    for pair in range(PAIRS):
        there = cols(2 * pair, 2)
        last = HALO - 2 * pair
        if last > 0:
            out_ref[:, there] = near_ref[:, there] + products(
                pair, 0, last, 0, mask_ref, ah, al, ath, atl, both, taper, ch, cl
            )
        else:
            out_ref[:, there] = near_ref[:, there]


def windowed(kernel, members, own, window, span, flops, name):
    return pl.pallas_call(
        kernel,
        out_shape=jax.ShapeDtypeStruct((members, OWN * TILE), F32),
        in_specs=[SMEM, VMEM, VMEM, VMEM] + [VMEM] * (name == "far"),
        out_specs=VMEM,
        scratch_shapes=[
            pltpu.VMEM((members, own * TILE), BF),
            pltpu.VMEM((members, own * TILE), BF),
            pltpu.VMEM((window * TILE, members), BF),
            pltpu.VMEM((window * TILE, members), BF),
            pltpu.VMEM((2 * members, window * TILE), BF),
            pltpu.VMEM((span * TILE, 2 * TILE), F32),
            pltpu.VMEM((2, span * TILE, 2 * TILE), BF),
            pltpu.VMEM((2, span * TILE, 2 * TILE), BF),
        ],
        compiler_params=pltpu.CompilerParams(vmem_limit_bytes=32 * MIB),
        cost_estimate=pl.CostEstimate(flops=flops, bytes_accessed=8_000_000, transcendentals=0),
        name=name,
    )


def copying(kernel, outs, ins, name):
    return pl.pallas_call(
        kernel,
        out_shape=outs,
        in_specs=ins,
        out_specs=jax.tree.map(lambda _: VMEM, outs),
        compiler_params=pltpu.CompilerParams(vmem_limit_bytes=14 * MIB),
        cost_estimate=pl.CostEstimate(flops=0, bytes_accessed=6_000_000, transcendentals=0),
        name=name,
    )


def keep_mask(neighbours, core, chip, half, regions, value):
    theirs = lax.ppermute(neighbours, "region", [(r, r ^ 1) for r in range(regions)])
    table = jnp.where((chip >= half) == (core == 1), neighbours, theirs)
    start = (chip % half) * CHIP + core * OWN
    lists = lax.dynamic_slice_in_dim(table, start, OWN, 0)
    tiles = neighbours.shape[0] * regions
    region = lax.axis_index("region")
    first = ((region // 2) * 2 + chip // half) * neighbours.shape[0] + start
    spot = (lists - first + HALO) % tiles
    spot = jnp.where(core == 0, spot, WINDOW - 1 - spot[::-1])
    own = jnp.arange(OWN, dtype=jnp.int32).reshape(PAIRS, 1, 2)
    window = own[:, :1, :1] + jnp.arange(SPAN, dtype=jnp.int32).reshape(1, SPAN, 1)
    keep = jnp.any(spot.reshape(PAIRS, 1, 2, -1) == window[..., None], axis=-1)
    keep = jnp.where(keep, value, 0.0).astype(F32)
    return jnp.repeat(keep, TILE, axis=2).reshape(PAIRS * SPAN, 2 * TILE)


def outward(chips, regions):
    pairs = []
    for chip in range(chips):
        for region in range(regions):
            plane, core = region // 2, region % 2
            place = (plane * chips + chip + (1 if core else -1)) % (chips * regions // 2)
            pairs.append((chip * regions + region, place % chips * regions + place // chips * 2 + 1 - core))
    return pairs


def shards(states, weights, obs_count, neighbours):
    chips = lax.axis_size("member")
    regions = lax.axis_size("region")
    rows, local = states.shape
    half = chips // 2
    core = lax.axis_index("region") % 2
    chip = lax.axis_index("member")
    swap = [(r, r ^ 1) for r in range(regions)]
    members = chips * rows
    flag = core.reshape(1)
    own = OWN * TILE

    scaled, sent = copying(
        send_kernel,
        (jax.ShapeDtypeStruct((rows, local), F32), jax.ShapeDtypeStruct((half, 2 * rows, own), F32)),
        [SMEM, SMEM, VMEM, VMEM],
        "send",
    )(flag, obs_count, states, weights)
    got = lax.ppermute(sent, "region", swap)
    operand = copying(
        merge_kernel,
        jax.ShapeDtypeStruct((chips, 2 * rows, own), F32),
        [SMEM, VMEM, VMEM, VMEM],
        "merge",
    )(flag, states, scaled, got)
    mask = keep_mask(neighbours, core, chip, half, regions, 1.0 / (members - 1.0))
    operand, mask = lax.optimization_barrier((operand, mask))
    mine = lax.all_to_all(operand, "member", split_axis=0, concat_axis=0, tiled=True)
    halo = lax.ppermute(mine[:, :, : HALO * TILE], ("member", "region"), outward(chips, regions))
    other = lax.ppermute(mine[:, :, own - HALO * TILE :], "region", swap)
    near = windowed(near_kernel, members, OWN, OWN + HALO, SPAN, 18_000_000_000, "near")(flag, mask, mine, other)
    total = windowed(far_kernel, members, HALO, HALO, HALO, 4_000_000_000, "far")(flag, mask, mine, halo, near)
    back = lax.all_to_all(total.reshape(chips, rows, own), "member", split_axis=0, concat_axis=0, tiled=True)
    got = lax.ppermute(jnp.where(core == 0, back[half:], back[:half]), "region", swap)
    return copying(
        place_kernel, jax.ShapeDtypeStruct((rows, local), F32), [SMEM, VMEM, VMEM], "place"
    )(flag, back, got)


def solution(mesh):
    placed = (P("member", "region"), P("member", "region"), P("region"), P("region", None))
    return jax.shard_map(
        shards, mesh=mesh, in_specs=placed, out_specs=P("member", "region"), check_vma=False
    )
```

```python
import jax
import jax.numpy as jnp
from jax import lax
from jax.experimental import pallas as pl
from jax.experimental.pallas import tpu as pltpu
from jax.sharding import PartitionSpec as P

TILE = 128
HALO = 8
OWN = 12
CHIP = 2 * OWN
WINDOW = OWN + 2 * HALO
PAIRS = OWN // 2
SPAN = 2 * HALO + 2
BF = jnp.bfloat16
F32 = jnp.float32
MIB = 1024 * 1024
SIDE = 4
VMEM = pl.BlockSpec(memory_space=pltpu.VMEM)
SMEM = pl.BlockSpec(memory_space=pltpu.SMEM)
HBM = pl.BlockSpec(memory_space=pltpu.HBM)


def snake(chip):
    y, x = chip // SIDE, chip % SIDE
    odd = y % 2
    return y * SIDE + odd * (SIDE - 1 - x) + (1 - odd) * x


def placed(q, count, odd):
    return jnp.where(odd, snake(count - 1 - q), snake(q))


def split(x):
    high = x.astype(BF)
    return high, (x - high.astype(F32)).astype(BF)


def dot(a, b):
    return jnp.dot(a, b, preferred_element_type=F32)


def cols(start, count=1):
    return slice(start * TILE, (start + count) * TILE)


def lanes(t, count=1):
    return pl.ds(pl.multiple_of(t * TILE, TILE), count * TILE)


def send_kernel(core_ref, counts_ref, states_hbm, weights_hbm, scaled_ref, out_ref, states_ref, weights_ref, sems):
    half = out_ref.shape[0]
    copies = [
        pltpu.make_async_copy(source, target, sems.at[i])
        for i, (source, target) in enumerate(((states_hbm, states_ref), (weights_hbm, weights_ref)))
    ]
    for copy in copies:
        copy.start()

    def scale():
        @pl.loop(0, half * CHIP // 8)
        def _(group):
            for lane in range(8):
                t = group * 8 + lane
                count = jnp.full((1, TILE), counts_ref[t], jnp.int32).astype(F32)
                scaled_ref[:, lanes(t)] = weights_ref[:, lanes(t)] * (count / (count + 8.0))

    rows = states_ref.shape[0]
    copies[0].wait()
    for ref, there in ((states_ref, slice(0, rows)), (scaled_ref, slice(rows, None))):
        if ref is scaled_ref:
            copies[1].wait()
            scale()

        @pl.when(core_ref[0] == 0)
        def _(ref=ref, there=there):
            for q in range(half):
                for t in range(OWN):
                    out_ref[q, there, cols(t)] = ref[:, cols((q + 1) * CHIP - 1 - t)]

        @pl.when(core_ref[0] != 0)
        def _(ref=ref, there=there):
            for q in range(half):
                out_ref[q, there, cols(0, OWN)] = ref[:, cols(q * CHIP, OWN)]


def merge_kernel(core_ref, odd_ref, states_ref, scaled_ref, got_ref, out_ref):
    half = got_ref.shape[0]
    rows = states_ref.shape[0]
    odd = odd_ref[0] != 0

    @pl.when(core_ref[0] == 0)
    def _():
        for q in range(half):
            there = placed(q, 2 * half, odd)
            out_ref[there, :rows, :] = states_ref[:, cols(q * CHIP, OWN)]
            out_ref[there, rows:, :] = scaled_ref[:, cols(q * CHIP, OWN)]
            out_ref[placed(half + q, 2 * half, odd)] = got_ref[q]

    @pl.when(core_ref[0] != 0)
    def _():
        for q in range(half):
            there = placed(half + q, 2 * half, odd)
            for t in range(OWN):
                out_ref[there, :rows, cols(t)] = states_ref[:, cols((q + 1) * CHIP - 1 - t)]
                out_ref[there, rows:, cols(t)] = scaled_ref[:, cols((q + 1) * CHIP - 1 - t)]
            out_ref[placed(q, 2 * half, odd)] = got_ref[q]


def place_kernel(core_ref, odd_ref, back_ref, got_ref, out_ref):
    half = got_ref.shape[0]
    odd = odd_ref[0] != 0

    @pl.when(core_ref[0] == 0)
    def _():
        for q in range(half):
            there, theirs = placed(q, 2 * half, odd), placed(q, half, odd)
            out_ref[:, cols(q * CHIP, OWN)] = back_ref[there]
            for t in range(OWN):
                out_ref[:, cols((q + 1) * CHIP - 1 - t)] = got_ref[theirs, :, cols(t)]

    @pl.when(core_ref[0] != 0)
    def _():
        for q in range(half):
            there, theirs = placed(half + q, 2 * half, odd), placed(q, half, odd)
            out_ref[:, cols(q * CHIP, OWN)] = got_ref[theirs]
            for t in range(OWN):
                out_ref[:, cols((q + 1) * CHIP - 1 - t)] = back_ref[there, :, cols(t)]


def anomaly_of(ref, t, members):
    rows = members // ref.shape[0]
    state = ref[:, :rows, lanes(t)].reshape(members, TILE)
    return state - jnp.sum(state, axis=0, keepdims=True) * (1.0 / members)


def place_window(ref, t, w, members, ath, atl, both):
    ath[lanes(w), :], atl[lanes(w), :] = split(anomaly_of(ref, t, members).T)
    weights = ref[:, members // ref.shape[0] :, lanes(t)].reshape(members, TILE)
    both[:members, lanes(w)], both[members:, lanes(w)] = split(weights)


def place_own(ref, t, members, ah, al):
    ah[:, lanes(t)], al[:, lanes(t)] = split(anomaly_of(ref, t, members))


def place_taper(core, count, taper):
    sign = jnp.where(core == 0, TILE, -TILE)

    @pl.loop(0, count)
    def _(k):
        down = lax.broadcasted_iota(jnp.int32, (TILE, 2 * TILE), 0)
        across = lax.broadcasted_iota(jnp.int32, (TILE, 2 * TILE), 1)
        second = (across >= TILE).astype(jnp.int32)
        spread = sign * (k - HALO - second) + down - (across - TILE * second)
        scaled = spread.astype(F32) / (2.0 * TILE)
        taper[lanes(k), :] = 1.0 / (1.0 + scaled * scaled)


def products(pair, first, last, skip, mask_ref, ah, al, ath, atl, both, taper, ch, cl):
    members = ah.shape[0]
    own_high, own_low = ah[:, cols(2 * pair, 2)], al[:, cols(2 * pair, 2)]
    slot = pair % 2
    for k in range(first, last, 2):
        there = cols(2 * pair + k - skip, 2)
        high = ath[there, :]
        covar = dot(high, own_high) + (dot(atl[there, :], own_high) + dot(high, own_low))
        covar = covar * taper[cols(k, 2), :]
        for half in range(2):
            keep = mask_ref[pair * SPAN + k + half : pair * SPAN + k + half + 1, :]
            coefficient = covar[half * TILE : (half + 1) * TILE] * keep
            ch[slot, cols(k + half), :], cl[slot, cols(k + half), :] = split(coefficient)
    band = cols(2 * pair + first - skip, last - first)
    high, low = ch[slot, cols(first, last - first), :], cl[slot, cols(first, last - first), :]
    total = dot(both[:, band], high)
    return total[:members] + (total[members:] + dot(both[:members, band], low))


def near_kernel(core_ref, mask_ref, mine_ref, other_ref, out_ref, ah, al, taper, ath, atl, both, ch, cl):
    members = ah.shape[0]

    @pl.loop(0, OWN)
    def _(t):
        place_window(mine_ref, t, t, members, ath, atl, both)
        place_own(mine_ref, t, members, ah, al)

    @pl.loop(0, HALO)
    def _(t):
        place_window(other_ref, t, OWN + HALO - 1 - t, members, ath, atl, both)

    place_taper(core_ref[0], SPAN, taper)
    for pair in range(PAIRS):
        first = max(0, HALO - 2 * pair)
        out_ref[:, cols(2 * pair, 2)] = products(
            pair, first, SPAN, HALO, mask_ref, ah, al, ath, atl, both, taper, ch, cl
        )


def far_kernel(mask_ref, halo_ref, near_ref, ah, al, taper, out_ref, ath, atl, both, ch, cl):
    members = ah.shape[0]

    @pl.loop(0, HALO)
    def _(t):
        place_window(halo_ref, t, HALO - 1 - t, members, ath, atl, both)

    out_ref[:, cols(HALO, OWN - HALO)] = near_ref[:, cols(HALO, OWN - HALO)]
    for pair in range(HALO // 2):
        there = cols(2 * pair, 2)
        out_ref[:, there] = near_ref[:, there] + products(
            pair, 0, HALO - 2 * pair, 0, mask_ref, ah, al, ath, atl, both, taper, ch, cl
        )


def windowed(kernel, members, window, span, outs, ins, flops, name):
    return pl.pallas_call(
        kernel,
        out_shape=outs,
        in_specs=ins,
        out_specs=jax.tree.map(lambda _: VMEM, outs),
        scratch_shapes=[
            pltpu.VMEM((window * TILE, members), BF),
            pltpu.VMEM((window * TILE, members), BF),
            pltpu.VMEM((2 * members, window * TILE), BF),
            pltpu.VMEM((2, span * TILE, 2 * TILE), BF),
            pltpu.VMEM((2, span * TILE, 2 * TILE), BF),
        ],
        compiler_params=pltpu.CompilerParams(vmem_limit_bytes=32 * MIB),
        cost_estimate=pl.CostEstimate(flops=flops, bytes_accessed=8_000_000, transcendentals=0),
        name=name,
    )


def copying(kernel, outs, ins, name, scratch=(), limit=14):
    return pl.pallas_call(
        kernel,
        out_shape=outs,
        in_specs=ins,
        out_specs=jax.tree.map(lambda _: VMEM, outs),
        scratch_shapes=scratch,
        compiler_params=pltpu.CompilerParams(vmem_limit_bytes=limit * MIB),
        cost_estimate=pl.CostEstimate(flops=0, bytes_accessed=6_000_000, transcendentals=0),
        name=name,
    )


def keep_mask(neighbours, core, chip, half, regions, value):
    theirs = lax.ppermute(neighbours, "region", [(r, r ^ 1) for r in range(regions)])
    table = jnp.where((chip >= half) == (core == 1), neighbours, theirs)
    start = (chip % half) * CHIP + core * OWN
    lists = lax.dynamic_slice_in_dim(table, start, OWN, 0)
    tiles = neighbours.shape[0] * regions
    region = lax.axis_index("region")
    first = ((region // 2) * 2 + chip // half) * neighbours.shape[0] + start
    spot = (lists - first + HALO) % tiles
    spot = jnp.where(core == 0, spot, WINDOW - 1 - spot[::-1])
    own = jnp.arange(OWN, dtype=jnp.int32).reshape(PAIRS, 1, 2)
    window = own[:, :1, :1] + jnp.arange(SPAN, dtype=jnp.int32).reshape(1, SPAN, 1)
    keep = jnp.any(spot.reshape(PAIRS, 1, 2, -1) == window[..., None], axis=-1)
    keep = jnp.where(keep, value, 0.0).astype(F32)
    return jnp.repeat(keep, TILE, axis=2).reshape(PAIRS * SPAN, 2 * TILE)


def outward(chips, regions):
    def order(plane, place):
        return snake(chips - 1 - place) if plane % 2 else snake(place)

    pairs = []
    for plane in range(regions // 2):
        for place in range(chips):
            for core in range(2):
                there, spot = divmod((plane * chips + place + (1 if core else -1)) % (chips * regions // 2), chips)
                source = order(plane, place) * regions + plane * 2 + core
                pairs.append((source, order(there, spot) * regions + there * 2 + 1 - core))
    return pairs


def shards(states, weights, obs_count, neighbours):
    chips = lax.axis_size("member")
    regions = lax.axis_size("region")
    rows, local = states.shape
    half = chips // 2
    core = lax.axis_index("region") % 2
    odd = lax.axis_index("region") // 2 % 2
    place = snake(lax.axis_index("member"))
    chip = jnp.where(odd == 1, chips - 1 - place, place)
    swap = [(r, r ^ 1) for r in range(regions)]
    members = chips * rows
    flag = core.reshape(1)
    flags = flag, odd.reshape(1)
    own = OWN * TILE

    scaled, sent = copying(
        send_kernel,
        (jax.ShapeDtypeStruct((rows, local), F32), jax.ShapeDtypeStruct((half, 2 * rows, own), F32)),
        [SMEM, SMEM, HBM, HBM],
        "send",
        [
            pltpu.VMEM(states.shape, F32),
            pltpu.VMEM(weights.shape, F32),
            pltpu.SemaphoreType.DMA((2,)),
        ],
        limit=60,
    )(flag, obs_count, states, weights)
    got = lax.ppermute(sent, "region", swap)
    operand = copying(
        merge_kernel,
        jax.ShapeDtypeStruct((chips, 2 * rows, own), F32),
        [SMEM, SMEM, VMEM, VMEM, VMEM],
        "merge",
    )(*flags, states, scaled, got)
    mask = keep_mask(neighbours, core, chip, half, regions, 1.0 / (members - 1.0))
    upper = core == odd
    operand, mask, upper = lax.optimization_barrier((operand, mask, upper))
    mine = lax.all_to_all(operand, "member", split_axis=0, concat_axis=0, tiled=True)
    halo = lax.ppermute(mine[:, :, : HALO * TILE], ("member", "region"), outward(chips, regions))
    other = lax.ppermute(mine[:, :, own - HALO * TILE :], "region", swap)
    total = jax.ShapeDtypeStruct((members, own), F32)
    half_own = jax.ShapeDtypeStruct((members, own), BF)
    tapers = jax.ShapeDtypeStruct((SPAN * TILE, 2 * TILE), F32)
    near, high, low, tapers = windowed(
        near_kernel,
        members,
        OWN + HALO,
        SPAN,
        (total, half_own, half_own, tapers),
        [SMEM, VMEM, VMEM, VMEM],
        18_000_000_000,
        "near",
    )(flag, mask, mine, other)
    total = windowed(
        far_kernel, members, HALO, HALO, total, [VMEM] * 6, 4_000_000_000, "far"
    )(mask, halo, near, high, low, tapers)
    back = lax.all_to_all(total.reshape(chips, rows, own), "member", split_axis=0, concat_axis=0, tiled=True)
    got = lax.ppermute(jnp.where(upper, back[half:], back[:half]), "region", swap)
    return copying(
        place_kernel, jax.ShapeDtypeStruct((rows, local), F32), [SMEM, SMEM, VMEM, VMEM], "place"
    )(*flags, back, got)


def solution(mesh):
    specs = (P("member", "region"), P("member", "region"), P("region"), P("region", None))
    return jax.shard_map(
        shards, mesh=mesh, in_specs=specs, out_specs=P("member", "region"), check_vma=False
    )
```

```python
import jax
import jax.numpy as jnp
from jax import lax
from jax.experimental import pallas as pl
from jax.experimental.pallas import tpu as pltpu
from jax.sharding import PartitionSpec as P

TILE = 128
HALO = 8
OWN = 12
CHIP = 2 * OWN
WINDOW = OWN + 2 * HALO
PAIRS = OWN // 2
SPAN = 2 * HALO + 2
BF = jnp.bfloat16
F32 = jnp.float32
MIB = 1024 * 1024
SIDE = 4
VMEM = pl.BlockSpec(memory_space=pltpu.VMEM)
SMEM = pl.BlockSpec(memory_space=pltpu.SMEM)
HBM = pl.BlockSpec(memory_space=pltpu.HBM)


def snake(chip):
    y, x = chip // SIDE, chip % SIDE
    odd = y % 2
    return y * SIDE + odd * (SIDE - 1 - x) + (1 - odd) * x


def placed(q, count, odd):
    return jnp.where(odd, snake(count - 1 - q), snake(q))


def split(x):
    high = x.astype(BF)
    return high, (x - high.astype(F32)).astype(BF)


def dot(a, b):
    return jnp.dot(a, b, preferred_element_type=F32)


def cols(start, count=1):
    return slice(start * TILE, (start + count) * TILE)


def lanes(t, count=1):
    return pl.ds(pl.multiple_of(t * TILE, TILE), count * TILE)


def send_kernel(core_ref, states_hbm, weights_hbm, out_ref, states_ref, weights_ref, sems):
    half = out_ref.shape[0]
    rows = states_ref.shape[0]
    parts = (
        (pltpu.make_async_copy(states_hbm, states_ref, sems.at[0]), states_ref, slice(0, rows)),
        (pltpu.make_async_copy(weights_hbm, weights_ref, sems.at[1]), weights_ref, slice(rows, None)),
    )
    for copy, _, _ in parts:
        copy.start()
    for copy, ref, there in parts:
        copy.wait()

        @pl.when(core_ref[0] == 0)
        def _(ref=ref, there=there):
            for q in range(half):
                for t in range(OWN):
                    out_ref[q, there, cols(t)] = ref[:, cols((q + 1) * CHIP - 1 - t)]

        @pl.when(core_ref[0] != 0)
        def _(ref=ref, there=there):
            for q in range(half):
                out_ref[q, there, cols(0, OWN)] = ref[:, cols(q * CHIP, OWN)]


def scale(ref, q, rows, counts_ref, first, step):
    for t in range(OWN):
        count = jnp.full((1, TILE), counts_ref[first + step * t], jnp.int32).astype(F32)
        ref[q, rows:, cols(t)] = ref[q, rows:, cols(t)] * (count / (count + 8.0))


def merge_kernel(core_ref, odd_ref, counts_ref, theirs_ref, states_ref, weights_ref, got_ref, out_ref):
    half = got_ref.shape[0]
    rows = states_ref.shape[0]
    odd = odd_ref[0] != 0

    @pl.when(core_ref[0] == 0)
    def _():
        for q in range(half):
            there = placed(q, 2 * half, odd)
            out_ref[there, :rows, :] = states_ref[:, cols(q * CHIP, OWN)]
            out_ref[there, rows:, :] = weights_ref[:, cols(q * CHIP, OWN)]
            scale(out_ref, there, rows, counts_ref, q * CHIP, 1)
            there = placed(half + q, 2 * half, odd)
            out_ref[there] = got_ref[q]
            scale(out_ref, there, rows, theirs_ref, q * CHIP, 1)

    @pl.when(core_ref[0] != 0)
    def _():
        for q in range(half):
            there = placed(half + q, 2 * half, odd)
            for t in range(OWN):
                out_ref[there, :rows, cols(t)] = states_ref[:, cols((q + 1) * CHIP - 1 - t)]
                out_ref[there, rows:, cols(t)] = weights_ref[:, cols((q + 1) * CHIP - 1 - t)]
            scale(out_ref, there, rows, counts_ref, (q + 1) * CHIP - 1, -1)
            there = placed(q, 2 * half, odd)
            out_ref[there] = got_ref[q]
            scale(out_ref, there, rows, theirs_ref, (q + 1) * CHIP - 1, -1)


def place_kernel(core_ref, odd_ref, back_ref, got_ref, out_ref):
    half = got_ref.shape[0]
    odd = odd_ref[0] != 0

    @pl.when(core_ref[0] == 0)
    def _():
        for q in range(half):
            there, theirs = placed(q, 2 * half, odd), placed(q, half, odd)
            out_ref[:, cols(q * CHIP, OWN)] = back_ref[there]
            for t in range(OWN):
                out_ref[:, cols((q + 1) * CHIP - 1 - t)] = got_ref[theirs, :, cols(t)]

    @pl.when(core_ref[0] != 0)
    def _():
        for q in range(half):
            there, theirs = placed(half + q, 2 * half, odd), placed(q, half, odd)
            out_ref[:, cols(q * CHIP, OWN)] = got_ref[theirs]
            for t in range(OWN):
                out_ref[:, cols((q + 1) * CHIP - 1 - t)] = back_ref[there, :, cols(t)]


def anomaly_of(ref, t, members):
    rows = members // ref.shape[0]
    state = ref[:, :rows, lanes(t)].reshape(members, TILE)
    return state - jnp.sum(state, axis=0, keepdims=True) * (1.0 / members)


def place_window(ref, t, w, members, ath, atl, both):
    ath[lanes(w), :], atl[lanes(w), :] = split(anomaly_of(ref, t, members).T)
    weights = ref[:, members // ref.shape[0] :, lanes(t)].reshape(members, TILE)
    both[:members, lanes(w)], both[members:, lanes(w)] = split(weights)


def place_own(ref, t, members, ah, al):
    ah[:, lanes(t)], al[:, lanes(t)] = split(anomaly_of(ref, t, members))


def place_taper(core, count, taper):
    sign = jnp.where(core == 0, TILE, -TILE)

    @pl.loop(0, count)
    def _(k):
        down = lax.broadcasted_iota(jnp.int32, (TILE, 2 * TILE), 0)
        across = lax.broadcasted_iota(jnp.int32, (TILE, 2 * TILE), 1)
        second = (across >= TILE).astype(jnp.int32)
        spread = sign * (k - HALO - second) + down - (across - TILE * second)
        scaled = spread.astype(F32) / (2.0 * TILE)
        taper[lanes(k), :] = 1.0 / (1.0 + scaled * scaled)


def products(pair, first, last, skip, mask_ref, ah, al, ath, atl, both, taper, ch, cl):
    members = ah.shape[0]
    own_high, own_low = ah[:, cols(2 * pair, 2)], al[:, cols(2 * pair, 2)]
    slot = pair % 2
    for k in range(first, last, 2):
        there = cols(2 * pair + k - skip, 2)
        high = ath[there, :]
        covar = dot(high, own_high) + (dot(atl[there, :], own_high) + dot(high, own_low))
        covar = covar * taper[cols(k, 2), :]
        for half in range(2):
            keep = mask_ref[pair * SPAN + k + half : pair * SPAN + k + half + 1, :]
            coefficient = covar[half * TILE : (half + 1) * TILE] * keep
            ch[slot, cols(k + half), :], cl[slot, cols(k + half), :] = split(coefficient)
    band = cols(2 * pair + first - skip, last - first)
    high, low = ch[slot, cols(first, last - first), :], cl[slot, cols(first, last - first), :]
    total = dot(both[:, band], high)
    return total[:members] + (total[members:] + dot(both[:members, band], low))


def near_kernel(core_ref, mask_ref, mine_ref, other_ref, out_ref, ah, al, taper, ath, atl, both, ch, cl):
    members = ah.shape[0]

    @pl.loop(0, OWN)
    def _(t):
        place_window(mine_ref, t, t, members, ath, atl, both)
        place_own(mine_ref, t, members, ah, al)

    @pl.loop(0, HALO)
    def _(t):
        place_window(other_ref, t, OWN + HALO - 1 - t, members, ath, atl, both)

    place_taper(core_ref[0], SPAN, taper)
    for pair in range(PAIRS):
        first = max(0, HALO - 2 * pair)
        out_ref[:, cols(2 * pair, 2)] = products(
            pair, first, SPAN, HALO, mask_ref, ah, al, ath, atl, both, taper, ch, cl
        )


def far_kernel(mask_ref, halo_ref, near_ref, ah, al, taper, out_ref, ath, atl, both, ch, cl):
    members = ah.shape[0]

    @pl.loop(0, HALO)
    def _(t):
        place_window(halo_ref, t, HALO - 1 - t, members, ath, atl, both)

    out_ref[:, cols(HALO, OWN - HALO)] = near_ref[:, cols(HALO, OWN - HALO)]
    for pair in range(HALO // 2):
        there = cols(2 * pair, 2)
        out_ref[:, there] = near_ref[:, there] + products(
            pair, 0, HALO - 2 * pair, 0, mask_ref, ah, al, ath, atl, both, taper, ch, cl
        )


def windowed(kernel, members, window, span, outs, ins, flops, name):
    return pl.pallas_call(
        kernel,
        out_shape=outs,
        in_specs=ins,
        out_specs=jax.tree.map(lambda _: VMEM, outs),
        scratch_shapes=[
            pltpu.VMEM((window * TILE, members), BF),
            pltpu.VMEM((window * TILE, members), BF),
            pltpu.VMEM((2 * members, window * TILE), BF),
            pltpu.VMEM((2, span * TILE, 2 * TILE), BF),
            pltpu.VMEM((2, span * TILE, 2 * TILE), BF),
        ],
        compiler_params=pltpu.CompilerParams(vmem_limit_bytes=32 * MIB),
        cost_estimate=pl.CostEstimate(flops=flops, bytes_accessed=8_000_000, transcendentals=0),
        name=name,
    )


def copying(kernel, outs, ins, name, scratch=(), limit=14):
    return pl.pallas_call(
        kernel,
        out_shape=outs,
        in_specs=ins,
        out_specs=jax.tree.map(lambda _: VMEM, outs),
        scratch_shapes=scratch,
        compiler_params=pltpu.CompilerParams(vmem_limit_bytes=limit * MIB),
        cost_estimate=pl.CostEstimate(flops=0, bytes_accessed=6_000_000, transcendentals=0),
        name=name,
    )


def keep_mask(neighbours, core, chip, half, regions, value):
    theirs = lax.ppermute(neighbours, "region", [(r, r ^ 1) for r in range(regions)])
    table = jnp.where((chip >= half) == (core == 1), neighbours, theirs)
    start = (chip % half) * CHIP + core * OWN
    lists = lax.dynamic_slice_in_dim(table, start, OWN, 0)
    tiles = neighbours.shape[0] * regions
    region = lax.axis_index("region")
    first = ((region // 2) * 2 + chip // half) * neighbours.shape[0] + start
    spot = (lists - first + HALO) % tiles
    spot = jnp.where(core == 0, spot, WINDOW - 1 - spot[::-1])
    own = jnp.arange(OWN, dtype=jnp.int32).reshape(PAIRS, 1, 2)
    window = own[:, :1, :1] + jnp.arange(SPAN, dtype=jnp.int32).reshape(1, SPAN, 1)
    keep = jnp.any(spot.reshape(PAIRS, 1, 2, -1) == window[..., None], axis=-1)
    keep = jnp.where(keep, value, 0.0).astype(F32)
    return jnp.repeat(keep, TILE, axis=2).reshape(PAIRS * SPAN, 2 * TILE)


def outward(chips, regions):
    def order(plane, place):
        return snake(chips - 1 - place) if plane % 2 else snake(place)

    pairs = []
    for plane in range(regions // 2):
        for place in range(chips):
            for core in range(2):
                there, spot = divmod((plane * chips + place + (1 if core else -1)) % (chips * regions // 2), chips)
                source = order(plane, place) * regions + plane * 2 + core
                pairs.append((source, order(there, spot) * regions + there * 2 + 1 - core))
    return pairs


def shards(states, weights, obs_count, neighbours):
    chips = lax.axis_size("member")
    regions = lax.axis_size("region")
    rows, local = states.shape
    half = chips // 2
    core = lax.axis_index("region") % 2
    odd = lax.axis_index("region") // 2 % 2
    place = snake(lax.axis_index("member"))
    chip = jnp.where(odd == 1, chips - 1 - place, place)
    swap = [(r, r ^ 1) for r in range(regions)]
    members = chips * rows
    flag = core.reshape(1)
    flags = flag, odd.reshape(1)
    own = OWN * TILE

    sent = copying(
        send_kernel,
        jax.ShapeDtypeStruct((half, 2 * rows, own), F32),
        [SMEM, HBM, HBM],
        "send",
        [pltpu.VMEM(states.shape, F32), pltpu.VMEM(weights.shape, F32), pltpu.SemaphoreType.DMA((2,))],
        limit=60,
    )(flag, states, weights)
    sent, obs_count, neighbours = lax.optimization_barrier((sent, obs_count, neighbours))
    got = lax.ppermute(sent, "region", swap)
    operand = copying(
        merge_kernel,
        jax.ShapeDtypeStruct((chips, 2 * rows, own), F32),
        [SMEM] * 4 + [VMEM] * 3,
        "merge",
    )(*flags, obs_count, lax.ppermute(obs_count, "region", swap), states, weights, got)
    mask = keep_mask(neighbours, core, chip, half, regions, 1.0 / (members - 1.0))
    upper = core == odd
    operand, mask, upper = lax.optimization_barrier((operand, mask, upper))
    mine = lax.all_to_all(operand, "member", split_axis=0, concat_axis=0, tiled=True)
    halo = lax.ppermute(mine[:, :, : HALO * TILE], ("member", "region"), outward(chips, regions))
    other = lax.ppermute(mine[:, :, own - HALO * TILE :], "region", swap)
    total = jax.ShapeDtypeStruct((members, own), F32)
    half_own = jax.ShapeDtypeStruct((members, own), BF)
    tapers = jax.ShapeDtypeStruct((SPAN * TILE, 2 * TILE), F32)
    near, high, low, tapers = windowed(
        near_kernel,
        members,
        OWN + HALO,
        SPAN,
        (total, half_own, half_own, tapers),
        [SMEM, VMEM, VMEM, VMEM],
        18_000_000_000,
        "near",
    )(flag, mask, mine, other)
    total = windowed(
        far_kernel, members, HALO, HALO, total, [VMEM] * 6, 4_000_000_000, "far"
    )(mask, halo, near, high, low, tapers)
    back = lax.all_to_all(total.reshape(chips, rows, own), "member", split_axis=0, concat_axis=0, tiled=True)
    got = lax.ppermute(jnp.where(upper, back[half:], back[:half]), "region", swap)
    return copying(
        place_kernel, jax.ShapeDtypeStruct((rows, local), F32), [SMEM, SMEM, VMEM, VMEM], "place"
    )(*flags, back, got)


def solution(mesh):
    specs = (P("member", "region"), P("member", "region"), P("region"), P("region", None))
    return jax.shard_map(
        shards, mesh=mesh, in_specs=specs, out_specs=P("member", "region"), check_vma=False
    )
```

```python
import jax
import jax.numpy as jnp
from jax import lax
from jax.experimental import pallas as pl
from jax.experimental.pallas import tpu as pltpu
from jax.sharding import PartitionSpec as P

TILE = 128
HALO = 8
OWN = 12
CHIP = 2 * OWN
WINDOW = OWN + 2 * HALO
PAIRS = OWN // 2
SPAN = 2 * HALO + 2
BF = jnp.bfloat16
F32 = jnp.float32
MIB = 1024 * 1024
SIDE = 4
VMEM = pl.BlockSpec(memory_space=pltpu.VMEM)
SMEM = pl.BlockSpec(memory_space=pltpu.SMEM)
HBM = pl.BlockSpec(memory_space=pltpu.HBM)


def snake(chip):
    y, x = chip // SIDE, chip % SIDE
    odd = y % 2
    return y * SIDE + odd * (SIDE - 1 - x) + (1 - odd) * x


def placed(q, count, odd):
    return jnp.where(odd, snake(count - 1 - q), snake(q))


def split(x):
    high = x.astype(BF)
    return high, (x - high.astype(F32)).astype(BF)


def dot(a, b):
    return jnp.dot(a, b, preferred_element_type=F32)


def cols(start, count=1):
    return slice(start * TILE, (start + count) * TILE)


def lanes(t, count=1):
    return pl.ds(pl.multiple_of(t * TILE, TILE), count * TILE)


def send_kernel(core_ref, states_hbm, weights_hbm, out_ref, states_ref, weights_ref, sems):
    half = out_ref.shape[0]
    rows = states_ref.shape[0]
    parts = (
        (pltpu.make_async_copy(states_hbm, states_ref, sems.at[0]), states_ref, slice(0, rows)),
        (pltpu.make_async_copy(weights_hbm, weights_ref, sems.at[1]), weights_ref, slice(rows, None)),
    )
    for copy, _, _ in parts:
        copy.start()
    for copy, ref, there in parts:
        copy.wait()

        @pl.when(core_ref[0] == 0)
        def _(ref=ref, there=there):
            for q in range(half):
                for t in range(OWN):
                    out_ref[q, there, cols(t)] = ref[:, cols((q + 1) * CHIP - 1 - t)]

        @pl.when(core_ref[0] != 0)
        def _(ref=ref, there=there):
            for q in range(half):
                out_ref[q, there, cols(0, OWN)] = ref[:, cols(q * CHIP, OWN)]


def scale(ref, q, rows, counts_ref, first, step):
    for t in range(OWN):
        count = jnp.full((1, TILE), counts_ref[first + step * t], jnp.int32).astype(F32)
        ref[q, rows:, cols(t)] = ref[q, rows:, cols(t)] * (count / (count + 8.0))


def merge_kernel(core_ref, odd_ref, counts_ref, theirs_ref, states_ref, weights_ref, got_ref, out_ref):
    half = got_ref.shape[0]
    rows = states_ref.shape[0]
    odd = odd_ref[0] != 0

    @pl.when(core_ref[0] == 0)
    def _():
        for q in range(half):
            there = placed(q, 2 * half, odd)
            out_ref[there, :rows, :] = states_ref[:, cols(q * CHIP, OWN)]
            out_ref[there, rows:, :] = weights_ref[:, cols(q * CHIP, OWN)]
            scale(out_ref, there, rows, counts_ref, q * CHIP, 1)
            there = placed(half + q, 2 * half, odd)
            out_ref[there] = got_ref[q]
            scale(out_ref, there, rows, theirs_ref, q * CHIP, 1)

    @pl.when(core_ref[0] != 0)
    def _():
        for q in range(half):
            there = placed(half + q, 2 * half, odd)
            for t in range(OWN):
                out_ref[there, :rows, cols(t)] = states_ref[:, cols((q + 1) * CHIP - 1 - t)]
                out_ref[there, rows:, cols(t)] = weights_ref[:, cols((q + 1) * CHIP - 1 - t)]
            scale(out_ref, there, rows, counts_ref, (q + 1) * CHIP - 1, -1)
            there = placed(q, 2 * half, odd)
            out_ref[there] = got_ref[q]
            scale(out_ref, there, rows, theirs_ref, (q + 1) * CHIP - 1, -1)


def place_kernel(core_ref, odd_ref, back_ref, got_ref, out_ref):
    half = got_ref.shape[0]
    odd = odd_ref[0] != 0

    @pl.when(core_ref[0] == 0)
    def _():
        for q in range(half):
            there, theirs = placed(q, 2 * half, odd), placed(q, half, odd)
            out_ref[:, cols(q * CHIP, OWN)] = back_ref[there]
            for t in range(OWN):
                out_ref[:, cols((q + 1) * CHIP - 1 - t)] = got_ref[theirs, :, cols(t)]

    @pl.when(core_ref[0] != 0)
    def _():
        for q in range(half):
            there, theirs = placed(half + q, 2 * half, odd), placed(q, half, odd)
            out_ref[:, cols(q * CHIP, OWN)] = got_ref[theirs]
            for t in range(OWN):
                out_ref[:, cols((q + 1) * CHIP - 1 - t)] = back_ref[there, :, cols(t)]


def anomaly_of(ref, t, members):
    rows = members // ref.shape[0]
    state = ref[:, :rows, lanes(t)].reshape(members, TILE)
    return state - jnp.sum(state, axis=0, keepdims=True) * (1.0 / members)


def place_anomaly(ref, t, w, members, ath, atl):
    ath[lanes(w), :], atl[lanes(w), :] = split(anomaly_of(ref, t, members).T)


def place_weights(ref, t, w, members, both):
    rows = members // ref.shape[0]
    weights = ref[:, ref.shape[1] - rows :, lanes(t)].reshape(members, TILE)
    both[:members, lanes(w)], both[members:, lanes(w)] = split(weights)


def place_own(ref, t, members, ah, al):
    ah[:, lanes(t)], al[:, lanes(t)] = split(anomaly_of(ref, t, members))


def place_taper(core, count, taper):
    sign = jnp.where(core == 0, TILE, -TILE)

    @pl.loop(0, count)
    def _(k):
        down = lax.broadcasted_iota(jnp.int32, (TILE, 2 * TILE), 0)
        across = lax.broadcasted_iota(jnp.int32, (TILE, 2 * TILE), 1)
        second = (across >= TILE).astype(jnp.int32)
        spread = sign * (k - HALO - second) + down - (across - TILE * second)
        scaled = spread.astype(F32) / (2.0 * TILE)
        taper[lanes(k), :] = 1.0 / (1.0 + scaled * scaled)


def coefficients(pair, first, last, skip, mask_ref, ah, al, ath, atl, taper, ch, cl, base):
    own_high, own_low = ah[:, cols(2 * pair, 2)], al[:, cols(2 * pair, 2)]
    for k in range(first, last, 2):
        there = cols(2 * pair + k - skip, 2)
        high = ath[there, :]
        covar = dot(high, own_high) + (dot(atl[there, :], own_high) + dot(high, own_low))
        covar = covar * taper[cols(k, 2), :]
        for half in range(2):
            keep = mask_ref[pair * SPAN + k + half : pair * SPAN + k + half + 1, :]
            spot = cols(base + k + half)
            ch[spot, :], cl[spot, :] = split(covar[half * TILE : (half + 1) * TILE] * keep)


def applied(pair, first, last, skip, both, ch, cl, base):
    members = both.shape[0] // 2
    band = cols(2 * pair + first - skip, last - first)
    there = cols(base + first, last - first)
    total = dot(both[:, band], ch[there, :])
    return total[:members] + (total[members:] + dot(both[:members, band], cl[there, :]))


def near_kernel(core_ref, mask_ref, mine_ref, other_ref, out_ref, ah, al, taper, ath, atl, both, ch, cl):
    members = ah.shape[0]

    @pl.loop(0, OWN)
    def _(t):
        place_anomaly(mine_ref, t, t, members, ath, atl)
        place_weights(mine_ref, t, t, members, both)
        place_own(mine_ref, t, members, ah, al)

    @pl.loop(0, HALO)
    def _(t):
        place_anomaly(other_ref, t, OWN + HALO - 1 - t, members, ath, atl)
        place_weights(other_ref, t, OWN + HALO - 1 - t, members, both)

    place_taper(core_ref[0], SPAN, taper)
    for pair in range(PAIRS):
        first, base = max(0, HALO - 2 * pair), pair % 2 * SPAN
        coefficients(pair, first, SPAN, HALO, mask_ref, ah, al, ath, atl, taper, ch, cl, base)
        out_ref[:, cols(2 * pair, 2)] = applied(pair, first, SPAN, HALO, both, ch, cl, base)


def far_kernel(mask_ref, halo_ref, ah, al, taper, ch, cl, ath, atl):
    members = ah.shape[0]

    @pl.loop(0, HALO)
    def _(t):
        place_anomaly(halo_ref, t, HALO - 1 - t, members, ath, atl)

    for pair in range(HALO // 2):
        coefficients(pair, 0, HALO - 2 * pair, 0, mask_ref, ah, al, ath, atl, taper, ch, cl, pair * HALO)


def add_kernel(halo_ref, near_ref, ch, cl, out_ref, both):
    members = out_ref.shape[0]

    @pl.loop(0, HALO)
    def _(t):
        place_weights(halo_ref, t, HALO - 1 - t, members, both)

    out_ref[:, cols(HALO, OWN - HALO)] = near_ref[:, cols(HALO, OWN - HALO)]
    for pair in range(HALO // 2):
        there = cols(2 * pair, 2)
        out_ref[:, there] = near_ref[:, there] + applied(pair, 0, HALO - 2 * pair, 0, both, ch, cl, pair * HALO)


def windowed(kernel, outs, ins, scratch, flops, name):
    return pl.pallas_call(
        kernel,
        out_shape=outs,
        in_specs=ins,
        out_specs=jax.tree.map(lambda _: VMEM, outs),
        scratch_shapes=[pltpu.VMEM(shape, BF) for shape in scratch],
        compiler_params=pltpu.CompilerParams(vmem_limit_bytes=32 * MIB),
        cost_estimate=pl.CostEstimate(flops=flops, bytes_accessed=8_000_000, transcendentals=0),
        name=name,
    )


def copying(kernel, outs, ins, name, scratch=(), limit=14):
    return pl.pallas_call(
        kernel,
        out_shape=outs,
        in_specs=ins,
        out_specs=jax.tree.map(lambda _: VMEM, outs),
        scratch_shapes=scratch,
        compiler_params=pltpu.CompilerParams(vmem_limit_bytes=limit * MIB),
        cost_estimate=pl.CostEstimate(flops=0, bytes_accessed=6_000_000, transcendentals=0),
        name=name,
    )


def keep_mask(neighbours, core, chip, half, regions, value):
    theirs = lax.ppermute(neighbours, "region", [(r, r ^ 1) for r in range(regions)])
    table = jnp.where((chip >= half) == (core == 1), neighbours, theirs)
    start = (chip % half) * CHIP + core * OWN
    lists = lax.dynamic_slice_in_dim(table, start, OWN, 0)
    tiles = neighbours.shape[0] * regions
    region = lax.axis_index("region")
    first = ((region // 2) * 2 + chip // half) * neighbours.shape[0] + start
    spot = (lists - first + HALO) % tiles
    spot = jnp.where(core == 0, spot, WINDOW - 1 - spot[::-1])
    own = jnp.arange(OWN, dtype=jnp.int32).reshape(PAIRS, 1, 2)
    window = own[:, :1, :1] + jnp.arange(SPAN, dtype=jnp.int32).reshape(1, SPAN, 1)
    keep = jnp.any(spot.reshape(PAIRS, 1, 2, -1) == window[..., None], axis=-1)
    keep = jnp.where(keep, value, 0.0).astype(F32)
    return jnp.repeat(keep, TILE, axis=2).reshape(PAIRS * SPAN, 2 * TILE)


def outward(chips, regions):
    def order(plane, place):
        return snake(chips - 1 - place) if plane % 2 else snake(place)

    pairs = []
    for plane in range(regions // 2):
        for place in range(chips):
            for core in range(2):
                there, spot = divmod((plane * chips + place + (1 if core else -1)) % (chips * regions // 2), chips)
                source = order(plane, place) * regions + plane * 2 + core
                pairs.append((source, order(there, spot) * regions + there * 2 + 1 - core))
    return pairs


def shards(states, weights, obs_count, neighbours):
    chips = lax.axis_size("member")
    regions = lax.axis_size("region")
    rows, local = states.shape
    half = chips // 2
    core = lax.axis_index("region") % 2
    odd = lax.axis_index("region") // 2 % 2
    place = snake(lax.axis_index("member"))
    chip = jnp.where(odd == 1, chips - 1 - place, place)
    swap = [(r, r ^ 1) for r in range(regions)]
    members = chips * rows
    flag = core.reshape(1)
    flags = flag, odd.reshape(1)
    own = OWN * TILE

    sent = copying(
        send_kernel,
        jax.ShapeDtypeStruct((half, 2 * rows, own), F32),
        [SMEM, HBM, HBM],
        "send",
        [pltpu.VMEM(states.shape, F32), pltpu.VMEM(weights.shape, F32), pltpu.SemaphoreType.DMA((2,))],
        limit=60,
    )(flag, states, weights)
    sent, obs_count, neighbours = lax.optimization_barrier((sent, obs_count, neighbours))
    got = lax.ppermute(sent, "region", swap)
    operand = copying(
        merge_kernel,
        jax.ShapeDtypeStruct((chips, 2 * rows, own), F32),
        [SMEM] * 4 + [VMEM] * 3,
        "merge",
    )(*flags, obs_count, lax.ppermute(obs_count, "region", swap), states, weights, got)
    mask = keep_mask(neighbours, core, chip, half, regions, 1.0 / (members - 1.0))
    upper = core == odd
    operand, mask, upper = lax.optimization_barrier((operand, mask, upper))
    mine = lax.all_to_all(operand, "member", split_axis=0, concat_axis=0, tiled=True)
    axes, out = ("member", "region"), outward(chips, regions)
    halo = lax.ppermute(mine[:, :rows, : HALO * TILE], axes, out)
    halo_weights = lax.ppermute(mine[:, rows:, : HALO * TILE], axes, out)
    other = lax.ppermute(mine[:, :, own - HALO * TILE :], "region", swap)
    total = jax.ShapeDtypeStruct((members, own), F32)
    half_own = jax.ShapeDtypeStruct((members, own), BF)
    tapers = jax.ShapeDtypeStruct((SPAN * TILE, 2 * TILE), F32)
    window = (OWN + HALO) * TILE
    near, high, low, tapers = windowed(
        near_kernel,
        (total, half_own, half_own, tapers),
        [SMEM, VMEM, VMEM, VMEM],
        [(window, members)] * 2 + [(2 * members, window)] + [(2 * SPAN * TILE, 2 * TILE)] * 2,
        18_000_000_000,
        "near",
    )(flag, mask, mine, other)
    coefficient = jax.ShapeDtypeStruct((HALO // 2 * HALO * TILE, 2 * TILE), BF)
    high, low = windowed(
        far_kernel,
        (coefficient, coefficient),
        [VMEM] * 5,
        [(HALO * TILE, members)] * 2,
        2_000_000_000,
        "far",
    )(mask, halo, high, low, tapers)
    total = windowed(
        add_kernel, total, [VMEM] * 4, [(2 * members, HALO * TILE)], 2_000_000_000, "add"
    )(halo_weights, near, high, low)
    back = lax.all_to_all(total.reshape(chips, rows, own), "member", split_axis=0, concat_axis=0, tiled=True)
    got = lax.ppermute(jnp.where(upper, back[half:], back[:half]), "region", swap)
    return copying(
        place_kernel, jax.ShapeDtypeStruct((rows, local), F32), [SMEM, SMEM, VMEM, VMEM], "place"
    )(*flags, back, got)


def solution(mesh):
    specs = (P("member", "region"), P("member", "region"), P("region"), P("region", None))
    return jax.shard_map(
        shards, mesh=mesh, in_specs=specs, out_specs=P("member", "region"), check_vma=False
    )
```
